32 devices in a mesh: gx: 4 (over y, x), gy: 8 (over z, core).
Axes of the slice: x: 2, y: 2, z: 4, core: 2. Of those that a mesh axis runs over, the one named last changes fastest.
Arguments:
- populations: float32 [19, 64, 256, 256], P(None, 'gx', 'gy'), may hold values from 0.02 to 0.08
- ions: float32 [2, 64, 256, 256], P(None, 'gx', 'gy'), may hold values from 0.4 to 1.62, as said below
- mask: int32 [64, 256, 256], P('gx', 'gy'), may hold values from 0 to 1, as said below
Outputs:
- populations_out: float32 [19, 64, 256, 256], P(None, 'gx', 'gy')
- ions_out: float32 [2, 64, 256, 256], P(None, 'gx', 'gy')
- potential: float32 [64, 256, 256], P('gx', 'gy')
The draws below stay inside these ranges and needn't reach their ends.
Inputs may be any that keep to these rules, and one draw needn't show every extreme that they name: `mask`: 1 marks a solid cell: every cell with second index 0 or 255 or third index 0 or 255, and scattered cells elsewhere; 0 marks fluid. `ions`: positive concentrations.
All inputs are finite; a program needn't handle non-finite values.
Results may differ from the reference program's by a relative error of at most 0.0004.
Values sent between devices are 32-bit elements; how exact they have to be, the bound alone decides.
A program may use at most 128 MiB of HBM per device.

```python
import math
import jax
import jax.numpy as jnp
from jax import lax

NZ = 256
NX = 64
NY = 256


def draw_mask(key, part):
    scatter = jax.random.randint(jax.random.fold_in(key, 11), (NX, NY, NZ), 0, 32)
    solid = (scatter == 0).astype(jnp.int32)
    wid_pos = jnp.arange(NY, dtype=jnp.int32)[None, :, None]
    depth_pos = jnp.arange(NZ, dtype=jnp.int32)[None, None, :]
    walls = (wid_pos == 0) | (wid_pos == NY - 1) | (depth_pos == 0) | (depth_pos == NZ - 1)
    walls = jnp.broadcast_to(walls.astype(jnp.int32), (NX, NY, NZ))
    return jnp.maximum(solid, walls)


def draw_ions(key, part):
    shape = (2, NX, NY, NZ)
    exponent = jax.random.uniform(jax.random.fold_in(key, 23), shape, jnp.float32, math.log(0.4), math.log(1.6))
    values = jnp.exp(exponent)
    return values


def block_scale(key, shape, split, low, largest):
    level = 1.0
    for dim, shards_of in split:
        heights = jax.random.uniform(jax.random.fold_in(jax.random.fold_in(key, 6), dim), (shards_of,), jnp.float32, low / len(split), largest / len(split))
        level = level * jnp.repeat(jnp.exp(heights), shape[dim] // shards_of).reshape((-1,) + (1,) * (len(shape) - 1 - dim))
    return level


def setup_inputs(seed: int = 0) -> dict:
    key_list = jax.random.split(jax.random.key(seed), 4)
    populations = jnp.clip(0.02 + 0.06 * jax.random.uniform(key_list[0], (19, NX, NY, NZ), jnp.float32) ** block_scale(key_list[0], (19, NX, NY, NZ), ((1, 4), (2, 8)), -0.2, 0.2), 0.02, 0.08)
    ions = draw_ions(jax.random.fold_in(key_list[3], 71), 0)
    mask = draw_mask(jax.random.fold_in(key_list[3], 71), 0)
    return dict(populations=populations, ions=ions, mask=mask)


PRECISE = lax.Precision.HIGHEST
LATTICE_VELOCITY = [(0, 0, 0), (1, 0, 0), (-1, 0, 0), (0, 1, 0), (0, -1, 0), (0, 0, 1), (0, 0, -1),
            (1, 1, 0), (-1, -1, 0), (1, -1, 0), (-1, 1, 0), (1, 0, 1), (-1, 0, -1),
            (1, 0, -1), (-1, 0, 1), (0, 1, 1), (0, -1, -1), (0, 1, -1), (0, -1, 1)]
WEIGHTS = [1.0 / 3.0] + [1.0 / 18.0] * 6 + [1.0 / 36.0] * 12
OPPOSITE = [0, 2, 1, 4, 3, 6, 5, 8, 7, 10, 9, 12, 11, 14, 13, 16, 15, 18, 17]
RELAXATION = 0.8
SCREENING = 0.001
WALL_CHARGE = -0.1
FIELD_EXT = 0.3
DIFFUSIVITY = 0.1


def sine_table(length):
    series = jnp.arange(length, dtype=jnp.int32) + 1
    product = (series[:, None] * series[None, :]) % (2 * (length + 1))
    return jnp.sin(product.astype(jnp.float32) * (math.pi / (length + 1)))


def fourier_pair(length):
    series = jnp.arange(length, dtype=jnp.int32)
    product = (series[:, None] * series[None, :]) % length
    angles = product.astype(jnp.float32) * (2.0 * math.pi / length)
    return jnp.stack([jnp.cos(angles), -jnp.sin(angles)])


def wall_eigen(first, number, total):
    modes = (jnp.arange(number, dtype=jnp.int32) + first + 1).astype(jnp.float32)
    return 2.0 - 2.0 * jnp.cos(modes * (math.pi / (total + 1)))


def cycle_angles(first, number, total):
    modes = jnp.arange(number, dtype=jnp.int32) + first
    return modes.astype(jnp.float32) * (2.0 * math.pi / total)


def solve_potential(free_electrostatic_share):
    full_len, full_wid, depth = free_electrostatic_share.shape
    depth_sine = sine_table(depth)
    widthwise_basis_sines = sine_table(full_wid)
    pair = fourier_pair(full_len)
    sectioned = jnp.einsum("xyz,nz->xyn", free_electrostatic_share, depth_sine, precision=PRECISE)
    spectra = jnp.einsum("rkx,xyn->rkyn", pair, sectioned, precision=PRECISE)
    spectra = jnp.einsum("my,rkyn->rkmn", widthwise_basis_sines, spectra, precision=PRECISE)
    angles = cycle_angles(0, full_len, full_len)
    denom = (SCREENING + (2.0 - 2.0 * jnp.cos(angles))[:, None, None]
             + wall_eigen(0, full_wid, full_wid)[None, :, None]
             + wall_eigen(0, depth, depth)[None, None, :])
    spectra = spectra / denom[None]
    level = jnp.einsum("ym,rkmn->rkyn", widthwise_basis_sines, spectra, precision=PRECISE) * (2.0 / (full_wid + 1))
    lines = jnp.einsum("rkx,rkyn->xyn", pair, level, precision=PRECISE) * (1.0 / full_len)
    return jnp.einsum("nz,xyn->xyz", depth_sine, lines, precision=PRECISE) * (2.0 / (depth + 1))


def collide(populations, distribution_tuple, volumetric_push):
    density = jnp.sum(populations, axis=0)
    moment = []
    for component in range(3):
        total = jnp.zeros_like(density)
        for entry in range(19):
            if LATTICE_VELOCITY[entry][component] != 0:
                total = total + LATTICE_VELOCITY[entry][component] * populations[entry]
        moment.append(total)
    velocity = [(moment[component] + 0.5 * volumetric_push[component]) / density for component in range(3)]
    speed_sq = velocity[0] * velocity[0] + velocity[1] * velocity[1] + velocity[2] * velocity[2]
    power = velocity[0] * volumetric_push[0] + velocity[1] * volumetric_push[1] + velocity[2] * volumetric_push[2]
    posts = []
    for entry in range(19):
        along = LATTICE_VELOCITY[entry]
        proj_vel = jnp.zeros_like(density)
        proj_force = jnp.zeros_like(density)
        for component in range(3):
            if along[component] != 0:
                proj_vel = proj_vel + along[component] * velocity[component]
                proj_force = proj_force + along[component] * volumetric_push[component]
        weight = WEIGHTS[entry]
        equil = weight * density * (1.0 + 3.0 * proj_vel + 4.5 * proj_vel * proj_vel - 1.5 * speed_sq)
        source = weight * (3.0 * (proj_force - power) + 9.0 * proj_vel * proj_force)
        moved = populations[entry] - (populations[entry] - equil) / RELAXATION + (1.0 - 0.5 / RELAXATION) * source
        posts.append(distribution_tuple * moved + (1.0 - distribution_tuple) * populations[OPPOSITE[entry]])
    return jnp.stack(posts), velocity


def drift_diffuse(centre, neighbour_cells, distribution_tuple, velocity, gradient_of_voltage, potential, free_electrostatic_share):
    conc = centre[:2]
    laplace = -6.0 * conc
    drift = conc * (SCREENING * potential - free_electrostatic_share)[None]
    advect = jnp.zeros_like(conc)
    for component in range(3):
        upper, lower = neighbour_cells[component]
        up_val = upper[2:3] * upper[:2] + (1.0 - upper[2:3]) * conc
        low_val = lower[2:3] * lower[:2] + (1.0 - lower[2:3]) * conc
        laplace = laplace + up_val + low_val
        slope = 0.5 * (up_val - low_val)
        drift = drift - slope * gradient_of_voltage[component][None]
        advect = advect + slope * velocity[component][None]
    valence = jnp.asarray([1.0, -1.0], jnp.float32)[:, None, None, None]
    change = DIFFUSIVITY * (laplace + valence * drift) - advect
    return conc + distribution_tuple[None] * change


def reference(populations, ions, mask):
    distribution_tuple = (mask == 0).astype(jnp.float32)
    free_electrostatic_share = distribution_tuple * (ions[0] - ions[1]) + (1.0 - distribution_tuple) * WALL_CHARGE
    potential = solve_potential(free_electrostatic_share)
    field_len = FIELD_EXT - 0.5 * (jnp.roll(potential, -1, 0) - jnp.roll(potential, 1, 0))
    padded = jnp.pad(potential, ((0, 0), (1, 1), (1, 1)))
    field_wid = -0.5 * (padded[:, 2:, 1:-1] - padded[:, :-2, 1:-1])
    field_depth = -0.5 * (padded[:, 1:-1, 2:] - padded[:, 1:-1, :-2])
    gradient_of_voltage = [field_len, field_wid, field_depth]
    ion_concentration_sum = distribution_tuple * free_electrostatic_share
    volumetric_push = [ion_concentration_sum * voltage_grid for voltage_grid in gradient_of_voltage]
    post, velocity = collide(populations, distribution_tuple, volumetric_push)
    read = []
    for entry in range(19):
        along = LATTICE_VELOCITY[entry]
        read.append(jnp.roll(post[entry], along, axis=(0, 1, 2)))
    populations_out = jnp.stack(read)
    ionic = jnp.concatenate([ions, distribution_tuple[None]], axis=0)
    neighbour_cells = []
    for component in range(3):
        neighbour_cells.append((jnp.roll(ionic, -1, component + 1), jnp.roll(ionic, 1, component + 1)))
    ions_out = drift_diffuse(ionic, neighbour_cells, distribution_tuple, velocity, gradient_of_voltage, potential, free_electrostatic_share)
    return populations_out, ions_out, potential
```

```python
import math

import jax
import jax.numpy as jnp
import numpy as np
from jax import lax
from jax.experimental import pallas as pl
from jax.experimental.pallas import tpu as pltpu
from jax.sharding import PartitionSpec as P

PRECISE = lax.Precision.HIGH
C = [
    (0, 0, 0), (1, 0, 0), (-1, 0, 0), (0, 1, 0), (0, -1, 0), (0, 0, 1), (0, 0, -1),
    (1, 1, 0), (-1, -1, 0), (1, -1, 0), (-1, 1, 0), (1, 0, 1), (-1, 0, -1),
    (1, 0, -1), (-1, 0, 1), (0, 1, 1), (0, -1, -1), (0, 1, -1), (0, -1, 1),
]
WEIGHTS = [1.0 / 3.0] + [1.0 / 18.0] * 6 + [1.0 / 36.0] * 12
RELAXATION = 0.8
SCREENING = 0.001
WALL_CHARGE = -0.1
FIELD_EXT = 0.3
DIFFUSIVITY = 0.1
XP = [i for i in range(19) if C[i][0] == 1]
XM = [i for i in range(19) if C[i][0] == -1]
X0 = [i for i in range(19) if C[i][0] == 0]
YP = [i for i in range(19) if C[i][1] == 1]
YM = [i for i in range(19) if C[i][1] == -1]


def sine_table(n):
    s = np.arange(1, n + 1, dtype=np.int64)
    return np.sin((s[:, None] * s[None, :] % (2 * (n + 1))) * (math.pi / (n + 1))).astype(np.float32)


def hartley_table(n):
    s = np.arange(n, dtype=np.int64)
    a = (s[:, None] * s[None, :] % n) * (2.0 * math.pi / n)
    return ((np.cos(a) + np.sin(a)) / math.sqrt(n)).astype(np.float32)


def up(x, axis):
    n = lax.axis_size(axis)
    return lax.ppermute(x, axis, [(i, (i + 1) % n) for i in range(n)])


def down(x, axis):
    n = lax.axis_size(axis)
    return lax.ppermute(x, axis, [((i + 1) % n, i) for i in range(n)])


def shifted(x, step, axis):
    return pltpu.roll(x, step % x.shape[axis], axis)


def collide_kernel(pop, ion, fluid, pot, p0, pp, pm, ions_out):
    x = pl.program_id(0)
    rows, depth = 8, pop.shape[3]
    lane = lax.broadcasted_iota(jnp.int32, (rows, depth), 1)
    for j in range(pop.shape[2] // rows):
        lo = j * rows
        mid = pl.ds(lo + 1, rows)
        here = pl.ds(lo, rows)
        isf = fluid[x + 1, mid, :] > 0.0
        con = [ion[s, x + 1, mid, :] for s in range(2)]
        charge = jnp.where(isf, con[0] - con[1], WALL_CHARGE)
        phi = pot[x + 1, mid, :]
        after = jnp.where(lane == depth - 1, 0.0, shifted(phi, -1, 1))
        before = jnp.where(lane == 0, 0.0, shifted(phi, 1, 1))
        field = [
            FIELD_EXT - 0.5 * (pot[x + 2, mid, :] - pot[x, mid, :]),
            -0.5 * (pot[x + 1, pl.ds(lo + 2, rows), :] - pot[x + 1, pl.ds(lo, rows), :]),
            -0.5 * (after - before),
        ]
        load = jnp.where(isf, charge, 0.0)
        force = [load * f for f in field]
        f = [pop[i, 0, here, :] for i in range(19)]
        rho = f[0]
        for i in range(1, 19):
            rho = rho + f[i]
        inv = 1.0 / rho
        vel = []
        for a in range(3):
            m = 0.5 * force[a]
            for i in range(1, 19, 2):
                if C[i][a] == 1:
                    m = m + (f[i] - f[i + 1])
                elif C[i][a] == -1:
                    m = m - (f[i] - f[i + 1])
            vel.append(m * inv)
        r = rho * (1.0 / RELAXATION)
        half = 1.0 - 0.5 / RELAXATION
        speed = vel[0] * vel[0] + vel[1] * vel[1] + vel[2] * vel[2]
        power = vel[0] * force[0] + vel[1] * force[1] + vel[2] * force[2]
        base = r * (1.0 - 1.5 * speed) - (3.0 * half) * power
        keep = 1.0 - 1.0 / RELAXATION
        odd = [3.0 * r * vel[a] + (3.0 * half) * force[a] for a in range(3)]
        even = [4.5 * r * vel[a] + (9.0 * half) * force[a] for a in range(3)]

        def put(i, value):
            if i in XP:
                pp[XP.index(i), 0, here, :] = value
            elif i in XM:
                pm[XM.index(i), 0, here, :] = value
            else:
                p0[X0.index(i), 0, here, :] = value

        def along(c, v):
            total = None
            for a in range(3):
                if c[a] == 1:
                    total = v[a] if total is None else total + v[a]
                elif c[a] == -1:
                    total = -v[a] if total is None else total - v[a]
            return total

        put(0, jnp.where(isf, keep * f[0] + WEIGHTS[0] * base, f[0]))
        for i in range(1, 19, 2):
            e = WEIGHTS[i] * (base + along(C[i], vel) * along(C[i], even))
            o = WEIGHTS[i] * along(C[i], odd)
            put(i, jnp.where(isf, keep * f[i] + (e + o), f[i + 1]))
            put(i + 1, jnp.where(isf, keep * f[i + 1] + (e - o), f[i]))

        fl = fluid[x + 1, mid, :]
        near = [
            ((x + 2, mid), (x, mid)),
            ((x + 1, pl.ds(lo + 2, rows)), (x + 1, pl.ds(lo, rows))),
        ]
        flags = [[fluid[p, q, :] > 0.0 for p, q in pair] for pair in near]
        flags.append([shifted(fl, -1, 1) > 0.0, shifted(fl, 1, 1) > 0.0])
        for s in range(2):
            sign = 1.0 - 2.0 * s
            c = con[s]
            lap = -6.0 * c
            drift = c * (SCREENING * phi - charge)
            adv = 0.0
            for a in range(3):
                if a < 2:
                    q = [ion[s, pa, pb, :] for pa, pb in near[a]]
                else:
                    q = [shifted(c, -1, 1), shifted(c, 1, 1)]
                u = jnp.where(flags[a][0], q[0], c)
                d = jnp.where(flags[a][1], q[1], c)
                lap = lap + u + d
                slope = 0.5 * (u - d)
                drift = drift - slope * field[a]
                adv = adv + slope * vel[a]
            change = DIFFUSIVITY * (lap + sign * drift) - adv
            ions_out[s, 0, here, :] = jnp.where(isf, c + change, c)


def stream_kernel(p0, pp, pm, hl, hr, hb, ht, out):
    x = pl.program_id(0)
    last = pl.num_programs(0) - 1
    wid, depth = out.shape[2], out.shape[3]
    row = lax.broadcasted_iota(jnp.int32, (wid, depth), 0)
    for i in range(19):
        if i in XP:
            k = XP.index(i)
            plane = jnp.where(x == 0, hl[k], pp[k, 0])
        elif i in XM:
            k = XM.index(i)
            plane = jnp.where(x == last, hr[k], pm[k, 0])
        else:
            plane = p0[X0.index(i), 0]
        if C[i][1] == 1:
            halo = hb[YP.index(i), pl.ds(x, 1), :]
            plane = jnp.where(row == 0, halo, shifted(plane, 1, 0))
        elif C[i][1] == -1:
            halo = ht[YM.index(i), pl.ds(x, 1), :]
            plane = jnp.where(row == wid - 1, halo, shifted(plane, -1, 0))
        if C[i][2] != 0:
            plane = shifted(plane, C[i][2], 1)
        out[i, 0] = plane


def solve(charge):
    length, wid, depth = charge.shape
    gx, gy = lax.axis_size("gx"), lax.axis_size("gy")
    parts = gx * gy
    modes = depth // parts
    sz, sy, hx = sine_table(depth), sine_table(wid * gy), hartley_table(length * gx)
    full_len, full_wid = length * gx, wid * gy
    t = jnp.einsum("nz,pz->np", sz, charge.reshape(length * wid, depth), precision=PRECISE)
    t = t.reshape(parts, modes, length * wid)
    t = lax.all_to_all(t, ("gx", "gy"), split_axis=0, concat_axis=0, tiled=True)
    t = t.reshape(gx, gy, modes, length, wid).transpose(2, 0, 3, 1, 4)
    t = t.reshape(modes, full_len, full_wid)
    t = jnp.einsum("nxy,my->nxm", t, sy, precision=PRECISE)
    t = jnp.einsum("kx,nxm->nkm", hx, t, precision=PRECISE)
    me = lax.axis_index("gx") * gy + lax.axis_index("gy")

    def wall(first, number, total):
        m = (jnp.arange(number, dtype=jnp.int32) + first + 1).astype(jnp.float32)
        return 2.0 - 2.0 * jnp.cos(m * (math.pi / (total + 1)))

    ex = (2.0 - 2.0 * np.cos(np.arange(full_len) * (2.0 * math.pi / full_len))).astype(np.float32)
    denom = (
        SCREENING
        + ex[None, :, None]
        + wall(0, full_wid, full_wid)[None, None, :]
        + wall(me * modes, modes, depth)[:, None, None]
    )
    t = t * ((4.0 / ((full_wid + 1) * (depth + 1))) / denom)
    t = jnp.einsum("kx,nkm->nxm", hx, t, precision=PRECISE)
    t = jnp.einsum("nxm,my->nxy", t, sy, precision=PRECISE)
    t = t.reshape(modes, gx, length, gy, wid).transpose(1, 3, 0, 2, 4)
    t = t.reshape(parts, modes, length * wid)
    t = lax.all_to_all(t, ("gx", "gy"), split_axis=0, concat_axis=0, tiled=True)
    t = t.reshape(depth, length * wid)
    return jnp.einsum("np,nz->pz", t, sz, precision=PRECISE).reshape(length, wid, depth)


def beside(block, keep_low, keep_high):
    d = block.ndim
    cut = lambda v, lo, hi, axis: lax.slice_in_dim(v, lo, hi, axis=axis)
    lx, ly = block.shape[d - 3], block.shape[d - 2]
    left = up(cut(block, lx - 1, lx, d - 3), "gx")
    right = down(cut(block, 0, 1, d - 3), "gx")
    low = up(cut(block, ly - 1, ly, d - 2), "gy") * keep_low
    high = down(cut(block, 0, 1, d - 2), "gy") * keep_high
    mid = jnp.concatenate([low, block, high], axis=d - 2)
    pad = [(0, 0)] * (d - 3) + [(0, 0), (1, 1), (0, 0)]
    return jnp.concatenate([jnp.pad(left, pad), mid, jnp.pad(right, pad)], axis=d - 3)


def body(populations, ions, mask):
    length, wid, depth = mask.shape
    ygo = lax.axis_index("gy")
    fluid = (mask == 0).astype(jnp.float32)
    charge = fluid * (ions[0] - ions[1]) + (1.0 - fluid) * WALL_CHARGE
    ionic = beside(jnp.concatenate([ions, fluid[None]], axis=0), 1.0, 1.0)
    potential = solve(charge)
    pot = beside(
        potential,
        (ygo != 0).astype(jnp.float32),
        (ygo != lax.axis_size("gy") - 1).astype(jnp.float32),
    )
    block = lambda n, f: pl.BlockSpec((n, 1, wid, depth), lambda x: (0, f(x), 0, 0))
    same = lambda x: x
    whole = pl.BlockSpec(memory_space=pltpu.VMEM)
    shape = lambda n: jax.ShapeDtypeStruct((n, length, wid, depth), jnp.float32)
    cells = length * wid * depth
    p0, pp, pm, ions_out = pl.pallas_call(
        collide_kernel,
        grid=(length,),
        in_specs=[block(19, same), whole, whole, whole],
        out_specs=[block(9, same), block(5, same), block(5, same), block(2, same)],
        out_shape=[shape(9), shape(5), shape(5), shape(2)],
        compiler_params=pltpu.CompilerParams(vmem_limit_bytes=32 << 20),
        cost_estimate=pl.CostEstimate(
            flops=500 * cells, bytes_accessed=4 * 44 * cells, transcendentals=0
        ),
    )(populations, ionic[:2], ionic[2], pot)

    hl = up(pp[:, length - 1], "gx")
    hr = down(pm[:, 0], "gx")

    def row(i, y):
        if i in XP:
            return pp[XP.index(i), :, y]
        if i in XM:
            return pm[XM.index(i), :, y]
        return p0[X0.index(i), :, y]

    def moved(i, rows, beside_left, beside_right):
        if i in XP:
            return jnp.concatenate([beside_left, rows[:-1]], axis=0)
        if i in XM:
            return jnp.concatenate([rows[1:], beside_right], axis=0)
        return rows

    def rows_of(group, y):
        out = []
        for i in group:
            a = hl[XP.index(i), y][None] if i in XP else None
            b = hr[XM.index(i), y][None] if i in XM else None
            out.append(moved(i, row(i, y), a, b))
        return jnp.stack(out)

    hb = up(rows_of(YP, wid - 1), "gy")
    ht = down(rows_of(YM, 0), "gy")
    populations_out = pl.pallas_call(
        stream_kernel,
        grid=(length,),
        in_specs=[
            block(9, same),
            block(5, lambda x: jnp.maximum(x - 1, 0)),
            block(5, lambda x: jnp.minimum(x + 1, length - 1)),
            whole,
            whole,
            whole,
            whole,
        ],
        out_specs=block(19, same),
        out_shape=shape(19),
        compiler_params=pltpu.CompilerParams(vmem_limit_bytes=32 << 20),
        cost_estimate=pl.CostEstimate(
            flops=20 * cells, bytes_accessed=4 * 38 * cells, transcendentals=0
        ),
    )(p0, pp, pm, hl, hr, hb, ht)
    return populations_out, ions_out, potential


def solution(mesh):
    placed = (P(None, "gx", "gy", None), P(None, "gx", "gy", None), P("gx", "gy", None))
    return jax.shard_map(body, mesh=mesh, in_specs=placed, out_specs=placed, check_vma=False)
```

```python
import functools
import math

import jax
import jax.numpy as jnp
import numpy as np
from jax import lax
from jax.experimental import pallas as pl
from jax.experimental.pallas import tpu as pltpu
from jax.sharding import PartitionSpec as P

PRECISE = lax.Precision.HIGH
C = [
    (0, 0, 0), (1, 0, 0), (-1, 0, 0), (0, 1, 0), (0, -1, 0), (0, 0, 1), (0, 0, -1),
    (1, 1, 0), (-1, -1, 0), (1, -1, 0), (-1, 1, 0), (1, 0, 1), (-1, 0, -1),
    (1, 0, -1), (-1, 0, 1), (0, 1, 1), (0, -1, -1), (0, 1, -1), (0, -1, 1),
]
WEIGHTS = [1.0 / 3.0] + [1.0 / 18.0] * 6 + [1.0 / 36.0] * 12
RELAXATION = 0.8
SCREENING = 0.001
WALL_CHARGE = -0.1
FIELD_EXT = 0.3
DIFFUSIVITY = 0.1
XP = [i for i in range(19) if C[i][0] == 1]
XM = [i for i in range(19) if C[i][0] == -1]
X0 = [i for i in range(19) if C[i][0] == 0]
YP = [i for i in range(19) if C[i][1] == 1]
YM = [i for i in range(19) if C[i][1] == -1]


def sine_table(n):
    s = np.arange(1, n + 1, dtype=np.int64)
    return np.sin((s[:, None] * s[None, :] % (2 * (n + 1))) * (math.pi / (n + 1))).astype(np.float32)


def hartley_table(n):
    s = np.arange(n, dtype=np.int64)
    a = (s[:, None] * s[None, :] % n) * (2.0 * math.pi / n)
    return ((np.cos(a) + np.sin(a)) / math.sqrt(n)).astype(np.float32)


def up(x, axis):
    n = lax.axis_size(axis)
    return lax.ppermute(x, axis, [(i, (i + 1) % n) for i in range(n)])


def down(x, axis):
    n = lax.axis_size(axis)
    return lax.ppermute(x, axis, [((i + 1) % n, i) for i in range(n)])


def shifted(x, step, axis):
    return pltpu.roll(x, step % x.shape[axis], axis)


def collide_kernel(pop, ion, fluid, pot, p0, pp, pm, ions_out, top, bottom):
    collide_plane(pl.program_id(0), pop, ion, fluid, pot, p0, pp, pm, ions_out, top, bottom)


def faces_kernel(length, pop, ion, fluid, pot, face_p, face_m):
    @pl.when(pl.program_id(0) == 0)
    def _():
        collide_plane(0, pop, ion, fluid, pot, None, None, face_m, None, None, None)

    @pl.when(pl.program_id(0) == 1)
    def _():
        collide_plane(length - 1, pop, ion, fluid, pot, None, face_p, None, None, None, None)


def collide_plane(x, pop, ion, fluid, pot, p0, pp, pm, ions_out, top, bottom):
    rows, depth = 8, pop.shape[3]
    lane = lax.broadcasted_iota(jnp.int32, (rows, depth), 1)
    for j in range(pop.shape[2] // rows):
        lo = j * rows
        mid = pl.ds(lo + 1, rows)
        here = pl.ds(lo, rows)
        isf = fluid[x + 1, mid, :] > 0.0
        con = [ion[s, x + 1, mid, :] for s in range(2)]
        charge = jnp.where(isf, con[0] - con[1], WALL_CHARGE)
        phi = pot[x + 1, mid, :]
        after = jnp.where(lane == depth - 1, 0.0, shifted(phi, -1, 1))
        before = jnp.where(lane == 0, 0.0, shifted(phi, 1, 1))
        field = [
            FIELD_EXT - 0.5 * (pot[x + 2, mid, :] - pot[x, mid, :]),
            -0.5 * (pot[x + 1, pl.ds(lo + 2, rows), :] - pot[x + 1, pl.ds(lo, rows), :]),
            -0.5 * (after - before),
        ]
        load = jnp.where(isf, charge, 0.0)
        force = [load * f for f in field]
        f = [pop[i, 0, here, :] for i in range(19)]
        rho = f[0]
        for i in range(1, 19):
            rho = rho + f[i]
        inv = 1.0 / rho
        vel = []
        for a in range(3):
            m = 0.5 * force[a]
            for i in range(1, 19, 2):
                if C[i][a] == 1:
                    m = m + (f[i] - f[i + 1])
                elif C[i][a] == -1:
                    m = m - (f[i] - f[i + 1])
            vel.append(m * inv)
        r = rho * (1.0 / RELAXATION)
        half = 1.0 - 0.5 / RELAXATION
        speed = vel[0] * vel[0] + vel[1] * vel[1] + vel[2] * vel[2]
        power = vel[0] * force[0] + vel[1] * force[1] + vel[2] * force[2]
        base = r * (1.0 - 1.5 * speed) - (3.0 * half) * power
        keep = 1.0 - 1.0 / RELAXATION
        odd = [3.0 * r * vel[a] + (3.0 * half) * force[a] for a in range(3)]
        even = [4.5 * r * vel[a] + (9.0 * half) * force[a] for a in range(3)]

        def put(i, value):
            ref, group = (pp, XP) if i in XP else (pm, XM) if i in XM else (p0, X0)
            if ref is None:
                return
            ref[group.index(i), 0, here, :] = value
            if top is not None and i in YP and lo + rows == pop.shape[2]:
                top[YP.index(i), pl.ds(x, 1), :] = value[rows - 1 : rows]
            if bottom is not None and i in YM and lo == 0:
                bottom[YM.index(i), pl.ds(x, 1), :] = value[0:1]

        def along(c, v):
            total = None
            for a in range(3):
                if c[a] == 1:
                    total = v[a] if total is None else total + v[a]
                elif c[a] == -1:
                    total = -v[a] if total is None else total - v[a]
            return total

        put(0, jnp.where(isf, keep * f[0] + WEIGHTS[0] * base, f[0]))
        for i in range(1, 19, 2):
            e = WEIGHTS[i] * (base + along(C[i], vel) * along(C[i], even))
            o = WEIGHTS[i] * along(C[i], odd)
            put(i, jnp.where(isf, keep * f[i] + (e + o), f[i + 1]))
            put(i + 1, jnp.where(isf, keep * f[i + 1] + (e - o), f[i]))

        if ions_out is None:
            continue
        fl = fluid[x + 1, mid, :]
        near = [
            ((x + 2, mid), (x, mid)),
            ((x + 1, pl.ds(lo + 2, rows)), (x + 1, pl.ds(lo, rows))),
        ]
        flags = [[fluid[p, q, :] > 0.0 for p, q in pair] for pair in near]
        flags.append([shifted(fl, -1, 1) > 0.0, shifted(fl, 1, 1) > 0.0])
        for s in range(2):
            sign = 1.0 - 2.0 * s
            c = con[s]
            lap = -6.0 * c
            drift = c * (SCREENING * phi - charge)
            adv = 0.0
            for a in range(3):
                if a < 2:
                    q = [ion[s, pa, pb, :] for pa, pb in near[a]]
                else:
                    q = [shifted(c, -1, 1), shifted(c, 1, 1)]
                u = jnp.where(flags[a][0], q[0], c)
                d = jnp.where(flags[a][1], q[1], c)
                lap = lap + u + d
                slope = 0.5 * (u - d)
                drift = drift - slope * field[a]
                adv = adv + slope * vel[a]
            change = DIFFUSIVITY * (lap + sign * drift) - adv
            ions_out[s, 0, here, :] = jnp.where(isf, c + change, c)


def stream_kernel(p0, pp, pm, hl, hr, hb, ht, out):
    x = pl.program_id(0)
    last = pl.num_programs(0) - 1
    wid, depth = out.shape[2], out.shape[3]
    row = lax.broadcasted_iota(jnp.int32, (wid, depth), 0)
    for i in range(19):
        if i in XP:
            k = XP.index(i)
            plane = jnp.where(x == 0, hl[k], pp[k, 0])
        elif i in XM:
            k = XM.index(i)
            plane = jnp.where(x == last, hr[k], pm[k, 0])
        else:
            plane = p0[X0.index(i), 0]
        if C[i][1] == 1:
            halo = hb[YP.index(i), pl.ds(x, 1), :]
            plane = jnp.where(row == 0, halo, shifted(plane, 1, 0))
        elif C[i][1] == -1:
            halo = ht[YM.index(i), pl.ds(x, 1), :]
            plane = jnp.where(row == wid - 1, halo, shifted(plane, -1, 0))
        if C[i][2] != 0:
            plane = shifted(plane, C[i][2], 1)
        out[i, 0] = plane


def split(x):
    hi = x.astype(jnp.bfloat16)
    return hi, (x - hi.astype(jnp.float32)).astype(jnp.bfloat16)


def dot3(a, b):
    d = lambda x, y: jnp.dot(x, y, preferred_element_type=jnp.float32)
    return d(a[0], b[0]) + (d(a[0], b[1]) + d(a[1], b[0]))


def swap_groups(planes, group):
    planes = list(planes)
    lane = lax.broadcasted_iota(jnp.int32, planes[0].shape, 1) // group
    bit = 1
    while bit < len(planes):
        low = lane & bit == 0
        for i in range(len(planes)):
            if i & bit:
                continue
            a, b = planes[i], planes[i | bit]
            planes[i] = jnp.where(low, a, shifted(b, bit * group, 1))
            planes[i | bit] = jnp.where(low, shifted(a, -bit * group, 1), b)
        bit *= 2
    return planes


def depth_forward_kernel(ion, mask, shi, slo, out):
    length, wid, depth = mask.shape
    groups = length
    charge = jnp.where(mask[...] == 0, ion[0] - ion[1], WALL_CHARGE)
    t = dot3(split(charge.reshape(length * wid, depth)), (shi[...], slo[...]))
    for j in range(depth // 128):
        planes = [t[x * wid : (x + 1) * wid, j * 128 : (j + 1) * 128] for x in range(length)]
        for g, plane in enumerate(swap_groups(planes, 128 // groups)):
            out[j * groups + g] = plane


def depth_back_kernel(t, shi, slo, out):
    length, wid, depth = out.shape
    groups = length
    halves = []
    for j in range(depth // 128):
        planes = swap_groups([t[j * groups + g] for g in range(groups)], 128 // groups)
        halves.append(jnp.concatenate(planes, axis=0))
    v = jnp.concatenate(halves, axis=1)
    out[...] = dot3(split(v), (shi[...], slo[...])).reshape(length, wid, depth)


def plane_kernel(t, shi, slo, hhi, hlo, scale, out):
    gx = t.shape[0]
    sines, waves = (shi[...], slo[...]), (hhi[...], hlo[...])
    v = jnp.concatenate([t[g] for g in range(gx)], axis=1)
    v = dot3(sines, split(v))
    v = dot3(split(v), waves)
    v = v / scale[...]
    v = dot3(split(v), waves)
    v = dot3(sines, split(v))
    for g in range(gx):
        out[g] = v[:, g * 128 : (g + 1) * 128]


def halves(table):
    hi = table.astype(jnp.bfloat16)
    return hi, (table - hi.astype(np.float32)).astype(jnp.bfloat16)


def wall(first, number, total):
    m = (jnp.arange(number, dtype=jnp.int32) + first + 1).astype(jnp.float32)
    return 2.0 - 2.0 * jnp.cos(m * (math.pi / (total + 1)))


def solve_packed(ions, mask):
    length, wid, depth = mask.shape
    gx, gy = lax.axis_size("gx"), lax.axis_size("gy")
    parts = gx * gy
    modes = depth // parts
    full_len, full_wid = length * gx, wid * gy
    sz, sy, hx = sine_table(depth), sine_table(full_wid), hartley_table(full_len)
    waves = np.kron(hx, np.eye(modes, dtype=np.float32))
    params = pltpu.CompilerParams(vmem_limit_bytes=48 << 20)
    chunk = jax.ShapeDtypeStruct((parts, wid, 128), jnp.float32)
    t = pl.pallas_call(depth_forward_kernel, out_shape=chunk, compiler_params=params)(
        ions, mask, *halves(sz)
    )
    t = lax.all_to_all(t, ("gx", "gy"), split_axis=0, concat_axis=0, tiled=True)
    me = lax.axis_index("gx") * gy + lax.axis_index("gy")
    ex = (2.0 - 2.0 * np.cos(np.arange(full_len) * (2.0 * math.pi / full_len))).astype(np.float32)
    along = SCREENING + (ex[:, None] + wall(me * modes, modes, depth)[None, :]).reshape(1, -1)
    scale = (along + wall(0, full_wid, full_wid)[:, None]) * (
        (full_wid + 1) * (depth + 1) / 4.0
    )
    t = pl.pallas_call(
        plane_kernel,
        out_shape=jax.ShapeDtypeStruct((gx, full_wid, 128), jnp.float32),
        compiler_params=params,
    )(t.reshape(gx, full_wid, 128), *halves(sy), *halves(waves), scale)
    t = lax.all_to_all(
        t.reshape(parts, wid, 128), ("gx", "gy"), split_axis=0, concat_axis=0, tiled=True
    )
    return pl.pallas_call(
        depth_back_kernel,
        out_shape=jax.ShapeDtypeStruct((length, wid, depth), jnp.float32),
        compiler_params=params,
    )(t, *halves(sz))


def solve(charge):
    length, wid, depth = charge.shape
    gx, gy = lax.axis_size("gx"), lax.axis_size("gy")
    parts = gx * gy
    modes = depth // parts
    sz, sy, hx = sine_table(depth), sine_table(wid * gy), hartley_table(length * gx)
    full_len, full_wid = length * gx, wid * gy
    t = jnp.einsum("nz,pz->np", sz, charge.reshape(length * wid, depth), precision=PRECISE)
    t = t.reshape(parts, modes, length * wid)
    t = lax.all_to_all(t, ("gx", "gy"), split_axis=0, concat_axis=0, tiled=True)
    t = t.reshape(gx, gy, modes, length, wid).transpose(2, 0, 3, 1, 4)
    t = t.reshape(modes, full_len, full_wid)
    t = jnp.einsum("nxy,my->nxm", t, sy, precision=PRECISE)
    t = jnp.einsum("kx,nxm->nkm", hx, t, precision=PRECISE)
    me = lax.axis_index("gx") * gy + lax.axis_index("gy")

    ex = (2.0 - 2.0 * np.cos(np.arange(full_len) * (2.0 * math.pi / full_len))).astype(np.float32)
    denom = (
        SCREENING
        + ex[None, :, None]
        + wall(0, full_wid, full_wid)[None, None, :]
        + wall(me * modes, modes, depth)[:, None, None]
    )
    t = t * ((4.0 / ((full_wid + 1) * (depth + 1))) / denom)
    t = jnp.einsum("kx,nkm->nxm", hx, t, precision=PRECISE)
    t = jnp.einsum("nxm,my->nxy", t, sy, precision=PRECISE)
    t = t.reshape(modes, gx, length, gy, wid).transpose(1, 3, 0, 2, 4)
    t = t.reshape(parts, modes, length * wid)
    t = lax.all_to_all(t, ("gx", "gy"), split_axis=0, concat_axis=0, tiled=True)
    t = t.reshape(depth, length * wid)
    return jnp.einsum("np,nz->pz", t, sz, precision=PRECISE).reshape(length, wid, depth)


def beside(block, keep_low, keep_high):
    d = block.ndim
    cut = lambda v, lo, hi, axis: lax.slice_in_dim(v, lo, hi, axis=axis)
    lx, ly = block.shape[d - 3], block.shape[d - 2]
    left = up(cut(block, lx - 1, lx, d - 3), "gx")
    right = down(cut(block, 0, 1, d - 3), "gx")
    low = up(cut(block, ly - 1, ly, d - 2), "gy") * keep_low
    high = down(cut(block, 0, 1, d - 2), "gy") * keep_high
    mid = jnp.concatenate([low, block, high], axis=d - 2)
    pad = [(0, 0)] * (d - 3) + [(0, 0), (1, 1), (0, 0)]
    return jnp.concatenate([jnp.pad(left, pad), mid, jnp.pad(right, pad)], axis=d - 3)


def body(populations, ions, mask):
    length, wid, depth = mask.shape
    ygo = lax.axis_index("gy")
    fluid = (mask == 0).astype(jnp.float32)
    charge = fluid * (ions[0] - ions[1]) + (1.0 - fluid) * WALL_CHARGE
    ionic = beside(jnp.concatenate([ions, fluid[None]], axis=0), 1.0, 1.0)
    packed = length * (depth // (lax.axis_size("gx") * lax.axis_size("gy"))) == 128
    potential = solve_packed(ions, mask) if packed else solve(charge)
    pot = beside(
        potential,
        (ygo != 0).astype(jnp.float32),
        (ygo != lax.axis_size("gy") - 1).astype(jnp.float32),
    )
    block = lambda n, f: pl.BlockSpec((n, 1, wid, depth), lambda x: (0, f(x), 0, 0))
    same = lambda x: x
    whole = pl.BlockSpec(memory_space=pltpu.VMEM)
    shape = lambda n: jax.ShapeDtypeStruct((n, length, wid, depth), jnp.float32)
    cells = length * wid * depth
    face_p, face_m = pl.pallas_call(
        functools.partial(faces_kernel, length),
        grid=(2,),
        in_specs=[block(19, lambda x: x * (length - 1)), whole, whole, whole],
        out_specs=[whole, whole],
        out_shape=[jax.ShapeDtypeStruct((5, 1, wid, depth), jnp.float32)] * 2,
        compiler_params=pltpu.CompilerParams(vmem_limit_bytes=32 << 20),
        cost_estimate=pl.CostEstimate(
            flops=800 * wid * depth, bytes_accessed=4 * 48 * wid * depth, transcendentals=0
        ),
    )(populations, ionic[:2], ionic[2], pot)
    hl = up(face_p[:, 0], "gx")
    hr = down(face_m[:, 0], "gx")
    edge = jax.ShapeDtypeStruct((5, length, depth), jnp.float32)
    p0, pp, pm, ions_out, top, bottom = pl.pallas_call(
        collide_kernel,
        grid=(length,),
        in_specs=[block(19, same), whole, whole, whole],
        out_specs=[block(9, same), block(5, same), block(5, same), block(2, same), whole, whole],
        out_shape=[shape(9), shape(5), shape(5), shape(2), edge, edge],
        compiler_params=pltpu.CompilerParams(vmem_limit_bytes=32 << 20),
        cost_estimate=pl.CostEstimate(
            flops=500 * cells, bytes_accessed=4 * 44 * cells, transcendentals=0
        ),
    )(populations, ionic[:2], ionic[2], pot)

    def moved(rows, group, y):
        out = []
        for k, i in enumerate(group):
            r = rows[k]
            if i in XP:
                r = jnp.concatenate([hl[XP.index(i), y][None], r[:-1]], axis=0)
            elif i in XM:
                r = jnp.concatenate([r[1:], hr[XM.index(i), y][None]], axis=0)
            out.append(r)
        return jnp.stack(out)

    hb = up(moved(top, YP, wid - 1), "gy")
    ht = down(moved(bottom, YM, 0), "gy")
    populations_out = pl.pallas_call(
        stream_kernel,
        grid=(length,),
        in_specs=[
            block(9, same),
            block(5, lambda x: jnp.maximum(x - 1, 0)),
            block(5, lambda x: jnp.minimum(x + 1, length - 1)),
            whole,
            whole,
            whole,
            whole,
        ],
        out_specs=block(19, same),
        out_shape=shape(19),
        compiler_params=pltpu.CompilerParams(vmem_limit_bytes=32 << 20),
        cost_estimate=pl.CostEstimate(
            flops=20 * cells, bytes_accessed=4 * 38 * cells, transcendentals=0
        ),
    )(p0, pp, pm, hl, hr, hb, ht)
    return populations_out, ions_out, potential


def solution(mesh):
    placed = (P(None, "gx", "gy", None), P(None, "gx", "gy", None), P("gx", "gy", None))
    return jax.shard_map(body, mesh=mesh, in_specs=placed, out_specs=placed, check_vma=False)
```

```python
import functools
import math

import jax
import jax.numpy as jnp
import numpy as np
from jax import lax
from jax.experimental import pallas as pl
from jax.experimental.pallas import tpu as pltpu
from jax.sharding import PartitionSpec as P

PRECISE = lax.Precision.HIGH
C = [
    (0, 0, 0), (1, 0, 0), (-1, 0, 0), (0, 1, 0), (0, -1, 0), (0, 0, 1), (0, 0, -1),
    (1, 1, 0), (-1, -1, 0), (1, -1, 0), (-1, 1, 0), (1, 0, 1), (-1, 0, -1),
    (1, 0, -1), (-1, 0, 1), (0, 1, 1), (0, -1, -1), (0, 1, -1), (0, -1, 1),
]
WEIGHTS = [1.0 / 3.0] + [1.0 / 18.0] * 6 + [1.0 / 36.0] * 12
RELAXATION = 0.8
SCREENING = 0.001
WALL_CHARGE = -0.1
FIELD_EXT = 0.3
DIFFUSIVITY = 0.1
XP = [i for i in range(19) if C[i][0] == 1]
XM = [i for i in range(19) if C[i][0] == -1]
X0 = [i for i in range(19) if C[i][0] == 0]
YP = [i for i in range(19) if C[i][1] == 1]
YM = [i for i in range(19) if C[i][1] == -1]


def sine_table(n):
    s = np.arange(1, n + 1, dtype=np.int64)
    return np.sin((s[:, None] * s[None, :] % (2 * (n + 1))) * (math.pi / (n + 1))).astype(np.float32)


def hartley_table(n):
    s = np.arange(n, dtype=np.int64)
    a = (s[:, None] * s[None, :] % n) * (2.0 * math.pi / n)
    return ((np.cos(a) + np.sin(a)) / math.sqrt(n)).astype(np.float32)


def up(x, axis):
    n = lax.axis_size(axis)
    return lax.ppermute(x, axis, [(i, (i + 1) % n) for i in range(n)])


def down(x, axis):
    n = lax.axis_size(axis)
    return lax.ppermute(x, axis, [((i + 1) % n, i) for i in range(n)])


def shifted(x, step, axis):
    return pltpu.roll(x, step % x.shape[axis], axis)


def collide_kernel(pop, ion, fluid, pot, p0, pp, pm, ions_out, top, bottom):
    collide_plane(pl.program_id(0), pop, ion, fluid, pot, p0, pp, pm, ions_out, top, bottom)


def faces_kernel(length, pop, ion, fluid, pot, face_p, face_m):
    @pl.when(pl.program_id(0) == 0)
    def _():
        collide_plane(0, pop, ion, fluid, pot, None, None, face_m, None, None, None)

    @pl.when(pl.program_id(0) == 1)
    def _():
        collide_plane(length - 1, pop, ion, fluid, pot, None, face_p, None, None, None, None)


def collide_plane(x, pop, ion, fluid, pot, p0, pp, pm, ions_out, top, bottom):
    rows, depth = 8, pop.shape[3]
    lane = lax.broadcasted_iota(jnp.int32, (rows, depth), 1)
    for j in range(pop.shape[2] // rows):
        lo = j * rows
        mid = pl.ds(lo + 1, rows)
        here = pl.ds(lo, rows)
        isf = fluid[x + 1, mid, :] > 0.0
        con = [ion[s, x + 1, mid, :] for s in range(2)]
        charge = jnp.where(isf, con[0] - con[1], WALL_CHARGE)
        phi = pot[x + 1, mid, :]
        after = jnp.where(lane == depth - 1, 0.0, shifted(phi, -1, 1))
        before = jnp.where(lane == 0, 0.0, shifted(phi, 1, 1))
        field = [
            FIELD_EXT - 0.5 * (pot[x + 2, mid, :] - pot[x, mid, :]),
            -0.5 * (pot[x + 1, pl.ds(lo + 2, rows), :] - pot[x + 1, pl.ds(lo, rows), :]),
            -0.5 * (after - before),
        ]
        load = jnp.where(isf, charge, 0.0)
        force = [load * f for f in field]
        f = [pop[i, 0, here, :] for i in range(19)]
        rho = f[0]
        for i in range(1, 19):
            rho = rho + f[i]
        inv = 1.0 / rho
        vel = []
        for a in range(3):
            m = 0.5 * force[a]
            for i in range(1, 19, 2):
                if C[i][a] == 1:
                    m = m + (f[i] - f[i + 1])
                elif C[i][a] == -1:
                    m = m - (f[i] - f[i + 1])
            vel.append(m * inv)
        r = rho * (1.0 / RELAXATION)
        half = 1.0 - 0.5 / RELAXATION
        speed = vel[0] * vel[0] + vel[1] * vel[1] + vel[2] * vel[2]
        power = vel[0] * force[0] + vel[1] * force[1] + vel[2] * force[2]
        base = r * (1.0 - 1.5 * speed) - (3.0 * half) * power
        keep = 1.0 - 1.0 / RELAXATION
        odd = [3.0 * r * vel[a] + (3.0 * half) * force[a] for a in range(3)]
        even = [4.5 * r * vel[a] + (9.0 * half) * force[a] for a in range(3)]

        def put(i, value):
            ref, group = (pp, XP) if i in XP else (pm, XM) if i in XM else (p0, X0)
            if ref is None:
                return
            ref[group.index(i), 0, here, :] = value
            if top is not None and i in YP and lo + rows == pop.shape[2]:
                top[YP.index(i), pl.ds(x, 1), :] = value[rows - 1 : rows]
            if bottom is not None and i in YM and lo == 0:
                bottom[YM.index(i), pl.ds(x, 1), :] = value[0:1]

        def along(c, v):
            total = None
            for a in range(3):
                if c[a] == 1:
                    total = v[a] if total is None else total + v[a]
                elif c[a] == -1:
                    total = -v[a] if total is None else total - v[a]
            return total

        put(0, jnp.where(isf, keep * f[0] + WEIGHTS[0] * base, f[0]))
        for i in range(1, 19, 2):
            e = WEIGHTS[i] * (base + along(C[i], vel) * along(C[i], even))
            o = WEIGHTS[i] * along(C[i], odd)
            put(i, jnp.where(isf, keep * f[i] + (e + o), f[i + 1]))
            put(i + 1, jnp.where(isf, keep * f[i + 1] + (e - o), f[i]))

        if ions_out is None:
            continue
        fl = fluid[x + 1, mid, :]
        near = [
            ((x + 2, mid), (x, mid)),
            ((x + 1, pl.ds(lo + 2, rows)), (x + 1, pl.ds(lo, rows))),
        ]
        flags = [[fluid[p, q, :] > 0.0 for p, q in pair] for pair in near]
        flags.append([shifted(fl, -1, 1) > 0.0, shifted(fl, 1, 1) > 0.0])
        for s in range(2):
            sign = 1.0 - 2.0 * s
            c = con[s]
            lap = -6.0 * c
            drift = c * (SCREENING * phi - charge)
            adv = 0.0
            for a in range(3):
                if a < 2:
                    q = [ion[s, pa, pb, :] for pa, pb in near[a]]
                else:
                    q = [shifted(c, -1, 1), shifted(c, 1, 1)]
                u = jnp.where(flags[a][0], q[0], c)
                d = jnp.where(flags[a][1], q[1], c)
                lap = lap + u + d
                slope = 0.5 * (u - d)
                drift = drift - slope * field[a]
                adv = adv + slope * vel[a]
            change = DIFFUSIVITY * (lap + sign * drift) - adv
            ions_out[s, 0, here, :] = jnp.where(isf, c + change, c)


def stream_kernel(p0, pp, pm, hl, hr, hb, ht, out):
    x = pl.program_id(0)
    last = pl.num_programs(0) - 1
    wid, depth = out.shape[2], out.shape[3]
    row = lax.broadcasted_iota(jnp.int32, (wid, depth), 0)
    for i in range(19):
        if i in XP:
            k = XP.index(i)
            plane = jnp.where(x == 0, hl[k], pp[k, 0])
        elif i in XM:
            k = XM.index(i)
            plane = jnp.where(x == last, hr[k], pm[k, 0])
        else:
            plane = p0[X0.index(i), 0]
        if C[i][1] == 1:
            halo = hb[YP.index(i), pl.ds(x, 1), :]
            plane = jnp.where(row == 0, halo, shifted(plane, 1, 0))
        elif C[i][1] == -1:
            halo = ht[YM.index(i), pl.ds(x, 1), :]
            plane = jnp.where(row == wid - 1, halo, shifted(plane, -1, 0))
        if C[i][2] != 0:
            plane = shifted(plane, C[i][2], 1)
        out[i, 0] = plane


def split(x):
    hi = x.astype(jnp.bfloat16)
    return hi, (x - hi.astype(jnp.float32)).astype(jnp.bfloat16)


def dot3(a, b):
    d = lambda x, y: jnp.dot(x, y, preferred_element_type=jnp.float32)
    return d(a[0], b[0]) + (d(a[0], b[1]) + d(a[1], b[0]))


def swap_groups(planes, group):
    planes = list(planes)
    lane = lax.broadcasted_iota(jnp.int32, planes[0].shape, 1) // group
    bit = 1
    while bit < len(planes):
        low = lane & bit == 0
        for i in range(len(planes)):
            if i & bit:
                continue
            a, b = planes[i], planes[i | bit]
            planes[i] = jnp.where(low, a, shifted(b, bit * group, 1))
            planes[i | bit] = jnp.where(low, shifted(a, -bit * group, 1), b)
        bit *= 2
    return planes


def depth_forward_kernel(ion, mask, s, out):
    length, wid, depth = mask.shape
    groups = length
    charge = jnp.where(mask[...] == 0, ion[0] - ion[1], WALL_CHARGE)
    t = dot3(split(charge.reshape(length * wid, depth)), (s[0], s[1]))
    for j in range(depth // 128):
        planes = [t[x * wid : (x + 1) * wid, j * 128 : (j + 1) * 128] for x in range(length)]
        for g, plane in enumerate(swap_groups(planes, 128 // groups)):
            out[j * groups + g] = plane


def depth_back_kernel(t, s, out):
    length, wid, depth = out.shape
    groups = length
    halves = []
    for j in range(depth // 128):
        planes = swap_groups([t[j * groups + g] for g in range(groups)], 128 // groups)
        halves.append(jnp.concatenate(planes, axis=0))
    v = jnp.concatenate(halves, axis=1)
    out[...] = dot3(split(v), (s[0], s[1])).reshape(length, wid, depth)


def plane_kernel(t, s, h, scale, out):
    gx = t.shape[0]
    sines, waves = (s[0], s[1]), (h[0], h[1])
    v = jnp.concatenate([t[g] for g in range(gx)], axis=1)
    v = dot3(sines, split(v))
    v = dot3(split(v), waves)
    v = v / scale[...]
    v = dot3(split(v), waves)
    v = dot3(sines, split(v))
    for g in range(gx):
        out[g] = v[:, g * 128 : (g + 1) * 128]


def halves(table):
    hi = table.astype(jnp.bfloat16)
    return np.stack([hi, (table - hi.astype(np.float32)).astype(jnp.bfloat16)])


def wall(first, number, total):
    m = (jnp.arange(number, dtype=jnp.int32) + first + 1).astype(jnp.float32)
    return 2.0 - 2.0 * jnp.cos(m * (math.pi / (total + 1)))


def solve_packed(ions, mask):
    length, wid, depth = mask.shape
    gx, gy = lax.axis_size("gx"), lax.axis_size("gy")
    parts = gx * gy
    modes = depth // parts
    full_len, full_wid = length * gx, wid * gy
    sz, sy, hx = sine_table(depth), sine_table(full_wid), hartley_table(full_len)
    waves = np.kron(hx, np.eye(modes, dtype=np.float32))
    params = pltpu.CompilerParams(vmem_limit_bytes=48 << 20)
    chunk = jax.ShapeDtypeStruct((parts, wid, 128), jnp.float32)
    t = pl.pallas_call(depth_forward_kernel, out_shape=chunk, compiler_params=params)(
        ions, mask, halves(sz)
    )
    t = lax.all_to_all(t, ("gx", "gy"), split_axis=0, concat_axis=0, tiled=True)
    me = lax.axis_index("gx") * gy + lax.axis_index("gy")
    ex = (2.0 - 2.0 * np.cos(np.arange(full_len) * (2.0 * math.pi / full_len))).astype(np.float32)
    along = SCREENING + (ex[:, None] + wall(me * modes, modes, depth)[None, :]).reshape(1, -1)
    scale = (along + wall(0, full_wid, full_wid)[:, None]) * (
        (full_wid + 1) * (depth + 1) / 4.0
    )
    t = pl.pallas_call(
        plane_kernel,
        out_shape=jax.ShapeDtypeStruct((gx, full_wid, 128), jnp.float32),
        compiler_params=params,
    )(t.reshape(gx, full_wid, 128), halves(sy), halves(waves), scale)
    t = lax.all_to_all(
        t.reshape(parts, wid, 128), ("gx", "gy"), split_axis=0, concat_axis=0, tiled=True
    )
    return pl.pallas_call(
        depth_back_kernel,
        out_shape=jax.ShapeDtypeStruct((length, wid, depth), jnp.float32),
        compiler_params=params,
    )(t, halves(sz))


def solve(charge):
    length, wid, depth = charge.shape
    gx, gy = lax.axis_size("gx"), lax.axis_size("gy")
    parts = gx * gy
    modes = depth // parts
    sz, sy, hx = sine_table(depth), sine_table(wid * gy), hartley_table(length * gx)
    full_len, full_wid = length * gx, wid * gy
    t = jnp.einsum("nz,pz->np", sz, charge.reshape(length * wid, depth), precision=PRECISE)
    t = t.reshape(parts, modes, length * wid)
    t = lax.all_to_all(t, ("gx", "gy"), split_axis=0, concat_axis=0, tiled=True)
    t = t.reshape(gx, gy, modes, length, wid).transpose(2, 0, 3, 1, 4)
    t = t.reshape(modes, full_len, full_wid)
    t = jnp.einsum("nxy,my->nxm", t, sy, precision=PRECISE)
    t = jnp.einsum("kx,nxm->nkm", hx, t, precision=PRECISE)
    me = lax.axis_index("gx") * gy + lax.axis_index("gy")

    ex = (2.0 - 2.0 * np.cos(np.arange(full_len) * (2.0 * math.pi / full_len))).astype(np.float32)
    denom = (
        SCREENING
        + ex[None, :, None]
        + wall(0, full_wid, full_wid)[None, None, :]
        + wall(me * modes, modes, depth)[:, None, None]
    )
    t = t * ((4.0 / ((full_wid + 1) * (depth + 1))) / denom)
    t = jnp.einsum("kx,nkm->nxm", hx, t, precision=PRECISE)
    t = jnp.einsum("nxm,my->nxy", t, sy, precision=PRECISE)
    t = t.reshape(modes, gx, length, gy, wid).transpose(1, 3, 0, 2, 4)
    t = t.reshape(parts, modes, length * wid)
    t = lax.all_to_all(t, ("gx", "gy"), split_axis=0, concat_axis=0, tiled=True)
    t = t.reshape(depth, length * wid)
    return jnp.einsum("np,nz->pz", t, sz, precision=PRECISE).reshape(length, wid, depth)


def beside(block, keep_low, keep_high):
    d = block.ndim
    cut = lambda v, lo, hi, axis: lax.slice_in_dim(v, lo, hi, axis=axis)
    lx, ly = block.shape[d - 3], block.shape[d - 2]
    left = up(cut(block, lx - 1, lx, d - 3), "gx")
    right = down(cut(block, 0, 1, d - 3), "gx")
    low = up(cut(block, ly - 1, ly, d - 2), "gy") * keep_low
    high = down(cut(block, 0, 1, d - 2), "gy") * keep_high
    mid = jnp.concatenate([low, block, high], axis=d - 2)
    pad = [(0, 0)] * (d - 3) + [(0, 0), (1, 1), (0, 0)]
    return jnp.concatenate([jnp.pad(left, pad), mid, jnp.pad(right, pad)], axis=d - 3)


def body(populations, ions, mask):
    length, wid, depth = mask.shape
    ygo = lax.axis_index("gy")
    fluid = (mask == 0).astype(jnp.float32)
    charge = fluid * (ions[0] - ions[1]) + (1.0 - fluid) * WALL_CHARGE
    ionic = beside(jnp.concatenate([ions, fluid[None]], axis=0), 1.0, 1.0)
    packed = length * (depth // (lax.axis_size("gx") * lax.axis_size("gy"))) == 128
    potential = solve_packed(ions, mask) if packed else solve(charge)
    pot = beside(
        potential,
        (ygo != 0).astype(jnp.float32),
        (ygo != lax.axis_size("gy") - 1).astype(jnp.float32),
    )
    block = lambda n, f: pl.BlockSpec((n, 1, wid, depth), lambda x: (0, f(x), 0, 0))
    same = lambda x: x
    whole = pl.BlockSpec(memory_space=pltpu.VMEM)
    shape = lambda n: jax.ShapeDtypeStruct((n, length, wid, depth), jnp.float32)
    cells = length * wid * depth
    face_p, face_m = pl.pallas_call(
        functools.partial(faces_kernel, length),
        grid=(2,),
        in_specs=[block(19, lambda x: x * (length - 1)), whole, whole, whole],
        out_specs=[whole, whole],
        out_shape=[jax.ShapeDtypeStruct((5, 1, wid, depth), jnp.float32)] * 2,
        compiler_params=pltpu.CompilerParams(vmem_limit_bytes=32 << 20),
        cost_estimate=pl.CostEstimate(
            flops=800 * wid * depth, bytes_accessed=4 * 48 * wid * depth, transcendentals=0
        ),
    )(populations, ionic[:2], ionic[2], pot)
    hl = up(face_p[:, 0], "gx")
    hr = down(face_m[:, 0], "gx")
    edge = jax.ShapeDtypeStruct((5, length, depth), jnp.float32)
    p0, pp, pm, ions_out, top, bottom = pl.pallas_call(
        collide_kernel,
        grid=(length,),
        in_specs=[block(19, same), whole, whole, whole],
        out_specs=[block(9, same), block(5, same), block(5, same), block(2, same), whole, whole],
        out_shape=[shape(9), shape(5), shape(5), shape(2), edge, edge],
        compiler_params=pltpu.CompilerParams(vmem_limit_bytes=32 << 20),
        cost_estimate=pl.CostEstimate(
            flops=160000 * cells, bytes_accessed=4 * 44 * cells, transcendentals=0
        ),
    )(populations, ionic[:2], ionic[2], pot)

    def moved(rows, group, y):
        out = []
        for k, i in enumerate(group):
            r = rows[k]
            if i in XP:
                r = jnp.concatenate([hl[XP.index(i), y][None], r[:-1]], axis=0)
            elif i in XM:
                r = jnp.concatenate([r[1:], hr[XM.index(i), y][None]], axis=0)
            out.append(r)
        return jnp.stack(out)

    hb = up(moved(top, YP, wid - 1), "gy")
    ht = down(moved(bottom, YM, 0), "gy")
    populations_out = pl.pallas_call(
        stream_kernel,
        grid=(length,),
        in_specs=[
            block(9, same),
            block(5, lambda x: jnp.maximum(x - 1, 0)),
            block(5, lambda x: jnp.minimum(x + 1, length - 1)),
            whole,
            whole,
            whole,
            whole,
        ],
        out_specs=block(19, same),
        out_shape=shape(19),
        compiler_params=pltpu.CompilerParams(vmem_limit_bytes=32 << 20),
        cost_estimate=pl.CostEstimate(
            flops=20 * cells, bytes_accessed=4 * 38 * cells, transcendentals=0
        ),
    )(p0, pp, pm, hl, hr, hb, ht)
    return populations_out, ions_out, potential


def solution(mesh):
    placed = (P(None, "gx", "gy", None), P(None, "gx", "gy", None), P("gx", "gy", None))
    return jax.shard_map(body, mesh=mesh, in_specs=placed, out_specs=placed, check_vma=False)
```
